32 devices in a mesh: dp: 8 (over z, core), mp: 4 (over y, x).
Axes of the slice: x: 2, y: 2, z: 4, core: 2. Of those that a mesh axis runs over, the one named last changes fastest.
Arguments:
- visual: bfloat16 [256, 8, 6144], P('dp', None, 'mp'), may hold values from -6 to 6
- vis_gain: float32 [6144], replicated, may hold values from 0.1 to 1.9
- text: bfloat16 [256, 8, 4096], P(None, 'dp'), may hold values from -6 to 6
- text_gain: float32 [4096], replicated, may hold values from 0.1 to 1.9
- query_weight: bfloat16 [4096, 4096], P(None, 'mp'), may hold values from -0.375 to 0.375
- key_weight: bfloat16 [6144, 4096], P(None, 'mp'), may hold values from -0.078125 to 0.078125
- value_weight: bfloat16 [6144, 4096], P(None, 'mp'), may hold values from -0.078125 to 0.078125
- out_weight: bfloat16 [4096, 4096], P('mp'), may hold values from -0.09375 to 0.09375
Outputs:
- mixed: bfloat16 [256, 8, 4096], P('mp', 'dp')
The draws below stay inside these ranges and needn't reach their ends.
All inputs are finite; a program needn't handle non-finite values.
Results may differ from the reference program's by a relative error of at most 0.015.
Values may be sent and summed in bfloat16 or wider, within the bound.
A program may use at most 128 MiB of HBM per device.

```python
import jax
import jax.numpy as jnp
from jax import lax

D_VIT = 6144
DEC = 4096
HEADS = 32
HEAD_DIM = 128
VIS = 256
TXT = 256
IMAGES = 8


def block_levels(stream_key, extent, pieces, low, high):
    def one(position, shards_of):
        heights = jax.random.uniform(jax.random.fold_in(jax.random.fold_in(stream_key, 6), position), (shards_of,), jnp.float32, low / len(pieces), high / len(pieces))
        return jnp.repeat(jnp.exp(heights), extent[position] // shards_of).reshape((-1,) + (1,) * (len(extent) - position - 1))

    factor_of = one(*pieces[0])
    for cut in pieces[1:]:
        factor_of = factor_of * one(*cut)
    return factor_of


def normal_values(stream_key, extent, width, bound, pieces=(), held_as=jnp.bfloat16):
    result = width * jax.random.normal(stream_key, extent, jnp.float32)
    if pieces:
        result = result * block_levels(stream_key, extent, pieces, -0.22, 0.18)
    return jnp.clip(result, -bound, bound).astype(held_as)


def setup_inputs(seed: int = 0) -> dict:
    key_of = jax.random.split(jax.random.key(seed), 9)
    visual = normal_values(key_of[0], (VIS, IMAGES, D_VIT), 1.0, 6.0, ((0, 8), (2, 4)))
    vis_gain = jnp.clip(1.0 + 0.18 * jax.random.normal(key_of[1], (D_VIT,), jnp.float32), 0.1, 1.9)
    text = normal_values(key_of[2], (TXT, IMAGES, DEC), 1.0, 6.0, ((1, 8),))
    text_gain = jnp.clip(1.0 + 0.18 * jax.random.normal(key_of[3], (DEC,), jnp.float32), 0.1, 1.9)
    query_weight = normal_values(key_of[4], (DEC, DEC), (DEC // 16) ** -0.5, 0.375, ((1, 4),))
    key_weight = normal_values(key_of[5], (D_VIT, DEC), D_VIT ** -0.5, 0.078125, ((1, 4),))
    value_weight = normal_values(key_of[6], (D_VIT, DEC), D_VIT ** -0.5, 0.078125, ((1, 4),))
    out_weight = normal_values(key_of[7], (DEC, DEC), DEC ** -0.5, 0.09375, ((0, 4),))
    return dict(visual=visual, vis_gain=vis_gain, text=text, text_gain=text_gain, query_weight=query_weight, key_weight=key_weight, value_weight=value_weight, out_weight=out_weight)


epsilon = 1e-06

def layer_norm(values, gain):
    average = lax.optimization_barrier(jnp.mean(values, axis=-1, keepdims=True))
    centred = values - average
    spread = lax.optimization_barrier(jnp.mean(centred * centred, axis=-1, keepdims=True))
    return centred * lax.rsqrt(spread + epsilon) * gain

def attend_image(operands):
    query_block, key_block, value_block = operands
    scores = jnp.einsum('thd,vhd->htv', query_block.astype(jnp.float32), key_block.astype(jnp.float32)) / jnp.sqrt(jnp.float32(HEAD_DIM))
    probs = jax.nn.softmax(scores, axis=-1).astype(jnp.bfloat16)
    return jnp.einsum('htv,vhd->thd', probs.astype(jnp.float32), value_block.astype(jnp.float32)).astype(jnp.bfloat16)

def reference(visual, vis_gain, text, text_gain, query_weight, key_weight, value_weight, out_weight):
    vis_norm = layer_norm(visual.astype(jnp.float32), vis_gain.astype(jnp.float32)).astype(jnp.bfloat16)
    flat_vis = vis_norm.reshape(VIS * IMAGES, D_VIT)
    keys = jnp.dot(flat_vis, key_weight, preferred_element_type=jnp.float32).astype(jnp.bfloat16)
    values = jnp.dot(flat_vis, value_weight, preferred_element_type=jnp.float32).astype(jnp.bfloat16)
    keys = keys.reshape(VIS, IMAGES, HEADS, HEAD_DIM).transpose(1, 0, 2, 3)
    values = values.reshape(VIS, IMAGES, HEADS, HEAD_DIM).transpose(1, 0, 2, 3)
    text_f = text.astype(jnp.float32)
    text_norm = (text_f * lax.rsqrt(lax.optimization_barrier(jnp.mean(text_f * text_f, axis=-1, keepdims=True)) + epsilon) * text_gain.astype(jnp.float32)).astype(jnp.bfloat16)
    queries = jnp.dot(text_norm.reshape(TXT * IMAGES, DEC), query_weight, preferred_element_type=jnp.float32).astype(jnp.bfloat16)
    queries = queries.reshape(TXT, IMAGES, HEADS, HEAD_DIM).transpose(1, 0, 2, 3)
    context = lax.map(attend_image, (queries, keys, values))
    context = context.transpose(1, 0, 2, 3).reshape(TXT * IMAGES, DEC)
    projected = jnp.dot(context, out_weight, preferred_element_type=jnp.float32).reshape(TXT, IMAGES, DEC)
    return (text_f + projected).astype(jnp.bfloat16)
```

```python
import functools

import jax
import jax.numpy as jnp
from jax import lax
from jax.experimental import pallas as pl
from jax.experimental.pallas import tpu as pltpu
from jax.sharding import PartitionSpec as P

DEC = 4096
HEAD_DIM = 128


epsilon = 1e-06


def layer_norm(values, gain):
    average = jnp.mean(values, axis=-1, keepdims=True)
    centred = values - average
    spread = jnp.mean(centred * centred, axis=-1, keepdims=True)
    return centred * lax.rsqrt(spread + epsilon) * gain


def plain_body(visual, vis_gain, text, text_gain, query_weight, key_weight, value_weight, out_weight):
    relayed = lax.all_to_all(visual, "dp", split_axis=1, concat_axis=0, tiled=True)
    vis_tokens, images_here, feature_count = relayed.shape
    full_width = feature_count * lax.axis_size("mp")
    vis_rows = vis_tokens * images_here
    kv_columns = key_weight.shape[1]
    whole = lax.all_gather(relayed, "mp", axis=2, tiled=True)
    normed = layer_norm(whole.astype(jnp.float32), vis_gain).astype(jnp.bfloat16)
    normed = normed.reshape(vis_rows, full_width)
    keys = jnp.dot(normed, key_weight, preferred_element_type=jnp.float32).astype(jnp.bfloat16)
    values = jnp.dot(normed, value_weight, preferred_element_type=jnp.float32).astype(jnp.bfloat16)
    heads_here = kv_columns // HEAD_DIM
    text_tokens = text.shape[0]
    text_f = text.astype(jnp.float32)
    text_norm = (
        text_f * lax.rsqrt(jnp.mean(text_f * text_f, axis=-1, keepdims=True) + epsilon) * text_gain
    ).astype(jnp.bfloat16)
    queries = jnp.dot(
        text_norm.reshape(text_tokens * images_here, DEC),
        query_weight,
        preferred_element_type=jnp.float32,
    ).astype(jnp.bfloat16)
    queries = queries.reshape(text_tokens, images_here, heads_here, HEAD_DIM)
    keys = keys.reshape(vis_tokens, images_here, heads_here, HEAD_DIM)
    values = values.reshape(vis_tokens, images_here, heads_here, HEAD_DIM)
    scores = jnp.einsum(
        "tihd,vihd->ihtv", queries, keys, preferred_element_type=jnp.float32
    ) / jnp.sqrt(jnp.float32(HEAD_DIM))
    probs = jax.nn.softmax(scores, axis=-1).astype(jnp.bfloat16)
    context = jnp.einsum(
        "ihtv,vihd->tihd", probs, values, preferred_element_type=jnp.float32
    ).astype(jnp.bfloat16)
    context = context.reshape(text_tokens * images_here, kv_columns)
    summed = lax.psum_scatter(
        jnp.dot(context, out_weight, preferred_element_type=jnp.float32).astype(jnp.bfloat16),
        "mp",
        scatter_dimension=0,
        tiled=True,
    ).astype(jnp.float32)
    tokens_here = text_tokens // lax.axis_size("mp")
    residual = lax.dynamic_slice_in_dim(text, lax.axis_index("mp") * tokens_here, tokens_here, 0)
    return (residual.astype(jnp.float32) + summed.reshape(tokens_here, images_here, DEC)).astype(
        jnp.bfloat16
    )


def flipped(index, mask):
    result, bit = index, 1
    while bit <= mask:
        if mask & bit:
            result = result + bit - 2 * bit * lax.rem(lax.div(index, bit), 2)
        bit *= 2
    return result


def fused_kernel(
    n, vis_ref, vis_gain_ref, text_gain_ref, text_hbm, wq_hbm, wk_hbm, wv_hbm, wo_hbm, out_ref,
    gathered, normed, text_ref, text_norm, wq, wk, wv, wo, queries, keys, values, context,
    partial, first_in, second_out, second_in,
    local_sem, z_send, z_recv, x_send, x_recv, y_send, y_recv, d_send, d_recv,
    s1_send, s1_recv, s2_send, s2_recv,
):
    d, m = lax.axis_index("dp"), lax.axis_index("mp")
    x, y = lax.rem(m, 2), lax.div(m, 2)
    xm, ym = m + 1 - 2 * x, m + 2 - 4 * y
    block, features = vis_ref.shape[1], vis_ref.shape[2]
    columns = queries.shape[1]
    chunks, _, _, out_rows, chunk = partial.shape

    loads = [
        pltpu.make_async_copy(source, target, local_sem.at[i])
        for i, (source, target) in enumerate(
            [(text_hbm, text_ref), (wq_hbm, wq), (wk_hbm, wk), (wv_hbm, wv), (wo_hbm, wo)]
        )
    ]
    for load in loads:
        load.start()

    barrier = pltpu.get_barrier_semaphore()
    peers = [(flipped(d, k), m) for k in range(1, n)] + [(d, xm), (d, ym)]
    for peer in peers:
        pl.semaphore_signal(barrier, inc=1, device_id=peer, device_id_type=pl.DeviceIdType.MESH)
    pl.semaphore_wait(barrier, len(peers))

    def send(source, target, send_sem, recv_sem, device):
        return pltpu.make_async_remote_copy(
            src_ref=source, dst_ref=target, send_sem=send_sem, recv_sem=recv_sem,
            device_id=device, device_id_type=pl.DeviceIdType.MESH,
        )

    def rows(k):
        return pl.ds(k * block, block)

    def z_copy(k):
        target = flipped(d, k)
        return send(
            vis_ref.at[target], gathered.at[m, rows(k)], z_send.at[k], z_recv.at[k], (target, m)
        )

    def x_copy(k):
        mine = gathered.at[m, rows(k)]
        return send(mine, mine, x_send.at[k], x_recv.at[k], (d, xm))

    def y_copy(k):
        mine = gathered.at[m, rows(k)]
        return send(mine, mine, y_send.at[k], y_recv.at[k], (d, ym))

    def relay(k):
        if k % 2 == 0:
            part = gathered.at[xm, rows(k)]
            return send(part, part, d_send.at[k], d_recv.at[k], (d, ym))
        part = gathered.at[ym, rows(k)]
        return send(part, part, d_send.at[k], d_recv.at[k], (d, xm))

    def spread(k):
        if k > 0:
            z_copy(k).wait_recv()
        x_copy(k).start()
        y_copy(k).start()

    def pass_on(k):
        (x_copy if k % 2 == 0 else y_copy)(k).wait_recv()
        relay(k).start()

    def normalize(k):
        (y_copy if k % 2 == 0 else x_copy)(k).wait_recv()
        relay(k).wait_recv()
        parts = gathered.shape[0]

        def piece(i, carry):
            here = pl.ds(pl.multiple_of(k * block + i * 16, 16), 16)
            total = jnp.zeros((16, 1), jnp.float32)
            for q in range(parts):
                total += jnp.sum(gathered[q, here].astype(jnp.float32), axis=-1, keepdims=True)
            average = total / (parts * features)
            spread_of = jnp.zeros((16, 1), jnp.float32)
            for q in range(parts):
                centred = gathered[q, here].astype(jnp.float32) - average
                spread_of += jnp.sum(centred * centred, axis=-1, keepdims=True)
            scale = lax.rsqrt(spread_of / (parts * features) + epsilon)
            for q in range(parts):
                span = slice(q * features, (q + 1) * features)
                centred = gathered[q, here].astype(jnp.float32) - average
                normed[here, span] = (centred * scale * vis_gain_ref[:, span]).astype(jnp.bfloat16)
            return carry

        lax.fori_loop(0, block // 16, piece, 0)

    gathered[m, rows(0)] = vis_ref[d]
    spread(0)
    for k in range(1, n):
        z_copy(k).start()

    tile = min(256, columns)
    tiles = columns // tile

    def tile_at(j):
        return pl.ds(pl.multiple_of(j * tile, tile), tile)

    def text_piece(i, carry):
        here = pl.ds(pl.multiple_of(i * 16, 16), 16)
        piece = text_ref[here].astype(jnp.float32)
        mean = jnp.mean(piece * piece, axis=-1, keepdims=True)
        text_norm[here] = (piece * lax.rsqrt(mean + epsilon) * text_gain_ref[...]).astype(
            jnp.bfloat16
        )
        return carry

    def query_tile(j, carry):
        queries[:, tile_at(j)] = jnp.dot(
            text_norm[...], wq[:, tile_at(j)], preferred_element_type=jnp.float32
        ).astype(jnp.bfloat16)
        return carry

    def kv_tiles(span):
        def one(j, carry):
            keys[span, tile_at(j)] = jnp.dot(
                normed[span], wk[:, tile_at(j)], preferred_element_type=jnp.float32
            ).astype(jnp.bfloat16)
            values[span, tile_at(j)] = jnp.dot(
                normed[span], wv[:, tile_at(j)], preferred_element_type=jnp.float32
            ).astype(jnp.bfloat16)
            return carry

        return one

    spread(1)
    loads[0].wait()
    lax.fori_loop(0, text_ref.shape[0] // 16, text_piece, 0)
    pass_on(0)
    for k in range(2, n):
        spread(k)
        pass_on(k - 1)
        if k == 2:
            loads[1].wait()
        lower, upper = (k - 2) * tiles // (n - 2), (k - 1) * tiles // (n - 2)
        if n == 2:
            lower, upper = 0, tiles
        if upper > lower:
            lax.fori_loop(lower, upper, query_tile, 0)
        if k >= n // 2 + 1:
            normalize(k - n // 2 - 1)
    if n == 2:
        loads[1].wait()
        lax.fori_loop(0, tiles, query_tile, 0)
    half = n // 2
    for k in range(half):
        if k < n // 2 + 1 and not (n > 2 and k <= n - 1 - n // 2 - 1):
            normalize(k)
    loads[2].wait()
    loads[3].wait()
    first, second = pl.ds(0, half * block), pl.ds(half * block, half * block)
    lax.fori_loop(0, tiles // 2, kv_tiles(first), 0)
    pass_on(n - 1)
    lax.fori_loop(tiles // 2, tiles, kv_tiles(first), 0)
    for k in range(half, n):
        normalize(k)
    lax.fori_loop(0, tiles, kv_tiles(second), 0)

    for h in range(columns // HEAD_DIM):
        span = slice(h * HEAD_DIM, (h + 1) * HEAD_DIM)
        scores = lax.dot_general(
            queries[:, span], keys[:, span], (((1,), (1,)), ((), ())),
            preferred_element_type=jnp.float32,
        ) * (HEAD_DIM ** -0.5)
        weights = jnp.exp(scores - jnp.max(scores, axis=-1, keepdims=True))
        total = jnp.sum(weights, axis=-1, keepdims=True)
        mixed = jnp.dot(
            weights.astype(jnp.bfloat16), values[:, span], preferred_element_type=jnp.float32
        )
        context[:, span] = (mixed / total).astype(jnp.bfloat16)

    loads[4].wait()

    def order(c):
        if c % 2 == 0:
            return x, y, (d, xm), (d, ym)
        return y, x, (d, ym), (d, xm)

    def first_copy(c):
        a, _, near, _ = order(c)
        return send(partial.at[c, 1 - a], first_in.at[c], s1_send.at[c], s1_recv.at[c], near)

    def second_copy(c):
        return send(second_out.at[c], second_in.at[c], s2_send.at[c], s2_recv.at[c], order(c)[3])

    def project(c):
        product = jnp.dot(
            context[...], wo[:, c * chunk : (c + 1) * chunk], preferred_element_type=jnp.float32
        ).astype(jnp.bfloat16)
        for r in range(4):
            a, b = (r % 2, r // 2) if c % 2 == 0 else (r // 2, r % 2)
            partial[c, a, b] = product[r * out_rows : (r + 1) * out_rows]
        first_copy(c).start()

    def turn(c):
        a, b, _, _ = order(c)
        first_copy(c).wait_recv()
        second_out[c] = (
            partial[c, a, 1 - b].astype(jnp.float32) + first_in[c, 1 - b].astype(jnp.float32)
        ).astype(jnp.bfloat16)
        second_copy(c).start()

    def finish(c):
        a, b, _, _ = order(c)
        second_copy(c).wait_recv()
        span = slice(c * chunk, (c + 1) * chunk)
        residual = text_ref[pl.ds(pl.multiple_of(m * out_rows, 16), out_rows), span]
        out_ref[:, span] = (
            residual.astype(jnp.float32)
            + partial[c, a, b].astype(jnp.float32)
            + first_in[c, b].astype(jnp.float32)
            + second_in[c].astype(jnp.float32)
        ).astype(jnp.bfloat16)

    for c in range(chunks):
        project(c)
        if c >= 3:
            turn(c - 3)
    for c in range(max(chunks - 3, 0), chunks):
        turn(c)
    for c in range(chunks):
        finish(c)

    for k in range(n):
        if k > 0:
            z_copy(k).wait_send()
        x_copy(k).wait_send()
        y_copy(k).wait_send()
        relay(k).wait_send()
    for c in range(chunks):
        first_copy(c).wait_send()
        second_copy(c).wait_send()


def fused_body(n, visual, vis_gain, text, text_gain, query_weight, key_weight, value_weight, out_weight):
    block, _, features = visual.shape
    tokens, _, width = text.shape
    columns = key_weight.shape[1]
    vis_rows, vis_width = block * n, features * 4
    out_rows = tokens // 4
    chunks = 8
    chunk = width // chunks
    bf16 = jnp.bfloat16
    sems = [pltpu.SemaphoreType.DMA((5,))]
    sems += [pltpu.SemaphoreType.DMA((n,))] * 8 + [pltpu.SemaphoreType.DMA((chunks,))] * 4
    vmem = pl.BlockSpec(memory_space=pltpu.VMEM)
    anywhere = pl.BlockSpec(memory_space=pl.ANY)
    result = pl.pallas_call(
        functools.partial(fused_kernel, n),
        out_shape=jax.ShapeDtypeStruct((out_rows, width), bf16),
        in_specs=[vmem] * 3 + [anywhere] * 5,
        out_specs=vmem,
        scratch_shapes=[
            pltpu.VMEM((4, vis_rows, features), bf16),
            pltpu.VMEM((vis_rows, vis_width), bf16),
            pltpu.VMEM((tokens, width), bf16),
            pltpu.VMEM((tokens, width), bf16),
            pltpu.VMEM(query_weight.shape, bf16),
            pltpu.VMEM(key_weight.shape, bf16),
            pltpu.VMEM(value_weight.shape, bf16),
            pltpu.VMEM(out_weight.shape, bf16),
            pltpu.VMEM((tokens, columns), bf16),
            pltpu.VMEM((vis_rows, columns), bf16),
            pltpu.VMEM((vis_rows, columns), bf16),
            pltpu.VMEM((tokens, columns), bf16),
            pltpu.VMEM((chunks, 2, 2, out_rows, chunk), bf16),
            pltpu.VMEM((chunks, 2, out_rows, chunk), bf16),
            pltpu.VMEM((chunks, out_rows, chunk), bf16),
            pltpu.VMEM((chunks, out_rows, chunk), bf16),
        ]
        + sems,
        compiler_params=pltpu.CompilerParams(
            collective_id=0, has_side_effects=True, vmem_limit_bytes=63 * 2**20
        ),
    )(
        jnp.transpose(visual, (1, 0, 2)),
        vis_gain.reshape(1, vis_width),
        text_gain.reshape(1, width),
        text.reshape(tokens, width),
        query_weight,
        key_weight,
        value_weight,
        out_weight,
    )
    return result.reshape(out_rows, 1, width)


def body(visual, *rest):
    n, groups = lax.axis_size("dp"), lax.axis_size("mp")
    text, columns = rest[1], rest[4].shape[1]
    block, images, features = visual.shape
    fits = (
        groups == 4
        and n >= 2
        and n & (n - 1) == 0
        and images == n
        and block % 16 == 0
        and features % 128 == 0
        and columns % HEAD_DIM == 0
        and (columns < 256 or columns % 256 == 0)
        and text.shape[0] % 64 == 0
        and text.shape[2] % 1024 == 0
    )
    if fits:
        return fused_body(n, visual, *rest)
    return plain_body(visual, *rest)


def solution(mesh):
    in_specs = (
        P("dp", None, "mp"),
        P(),
        P(None, "dp", None),
        P(),
        P(None, "mp"),
        P(None, "mp"),
        P(None, "mp"),
        P("mp", None),
    )
    out_specs = P("mp", "dp", None)
    return jax.shard_map(body, mesh=mesh, in_specs=in_specs, out_specs=out_specs, check_vma=False)
```

```python
import functools

import jax
import jax.numpy as jnp
from jax import lax
from jax.experimental import pallas as pl
from jax.experimental.pallas import tpu as pltpu
from jax.sharding import PartitionSpec as P

DEC = 4096
HEAD_DIM = 128


epsilon = 1e-06


def layer_norm(values, gain):
    average = jnp.mean(values, axis=-1, keepdims=True)
    centred = values - average
    spread = jnp.mean(centred * centred, axis=-1, keepdims=True)
    return centred * lax.rsqrt(spread + epsilon) * gain


def plain_body(visual, vis_gain, text, text_gain, query_weight, key_weight, value_weight, out_weight):
    relayed = lax.all_to_all(visual, "dp", split_axis=1, concat_axis=0, tiled=True)
    vis_tokens, images_here, feature_count = relayed.shape
    full_width = feature_count * lax.axis_size("mp")
    vis_rows = vis_tokens * images_here
    kv_columns = key_weight.shape[1]
    whole = lax.all_gather(relayed, "mp", axis=2, tiled=True)
    normed = layer_norm(whole.astype(jnp.float32), vis_gain).astype(jnp.bfloat16)
    normed = normed.reshape(vis_rows, full_width)
    keys = jnp.dot(normed, key_weight, preferred_element_type=jnp.float32).astype(jnp.bfloat16)
    values = jnp.dot(normed, value_weight, preferred_element_type=jnp.float32).astype(jnp.bfloat16)
    heads_here = kv_columns // HEAD_DIM
    text_tokens = text.shape[0]
    text_f = text.astype(jnp.float32)
    text_norm = (
        text_f * lax.rsqrt(jnp.mean(text_f * text_f, axis=-1, keepdims=True) + epsilon) * text_gain
    ).astype(jnp.bfloat16)
    queries = jnp.dot(
        text_norm.reshape(text_tokens * images_here, DEC),
        query_weight,
        preferred_element_type=jnp.float32,
    ).astype(jnp.bfloat16)
    queries = queries.reshape(text_tokens, images_here, heads_here, HEAD_DIM)
    keys = keys.reshape(vis_tokens, images_here, heads_here, HEAD_DIM)
    values = values.reshape(vis_tokens, images_here, heads_here, HEAD_DIM)
    scores = jnp.einsum(
        "tihd,vihd->ihtv", queries, keys, preferred_element_type=jnp.float32
    ) / jnp.sqrt(jnp.float32(HEAD_DIM))
    probs = jax.nn.softmax(scores, axis=-1).astype(jnp.bfloat16)
    context = jnp.einsum(
        "ihtv,vihd->tihd", probs, values, preferred_element_type=jnp.float32
    ).astype(jnp.bfloat16)
    context = context.reshape(text_tokens * images_here, kv_columns)
    summed = lax.psum_scatter(
        jnp.dot(context, out_weight, preferred_element_type=jnp.float32).astype(jnp.bfloat16),
        "mp",
        scatter_dimension=0,
        tiled=True,
    ).astype(jnp.float32)
    tokens_here = text_tokens // lax.axis_size("mp")
    residual = lax.dynamic_slice_in_dim(text, lax.axis_index("mp") * tokens_here, tokens_here, 0)
    return (residual.astype(jnp.float32) + summed.reshape(tokens_here, images_here, DEC)).astype(
        jnp.bfloat16
    )


def flipped(index, mask):
    result, bit = index, 1
    while bit <= mask:
        if mask & bit:
            result = result + bit - 2 * bit * lax.rem(lax.div(index, bit), 2)
        bit *= 2
    return result


def fused_kernel(
    n, vis_ref, vis_gain_ref, text_gain_ref, text_hbm, wq_hbm, wk_hbm, wv_hbm, wo_hbm, out_ref,
    gathered, normed, text_ref, text_norm, wq, wk, wv, wo, queries, keys, values, context,
    partial, first_in, second_out, second_in,
    local_sem, z_send, z_recv, x_send, x_recv, y_send, y_recv, d_send, d_recv,
    s1_send, s1_recv, s2_send, s2_recv,
):
    d, m = lax.axis_index("dp"), lax.axis_index("mp")
    x, y = lax.rem(m, 2), lax.div(m, 2)
    xm, ym = m + 1 - 2 * x, m + 2 - 4 * y
    block, features = vis_ref.shape[1], vis_ref.shape[2]
    columns = queries.shape[1]
    chunks, _, _, out_rows, chunk = partial.shape

    loads = [
        pltpu.make_async_copy(source, target, local_sem.at[i])
        for i, (source, target) in enumerate(
            [(text_hbm, text_ref), (wq_hbm, wq), (wk_hbm, wk), (wv_hbm, wv), (wo_hbm, wo)]
        )
    ]
    for load in loads:
        load.start()

    barrier = pltpu.get_barrier_semaphore()
    peers = [(flipped(d, k), m) for k in range(1, n)] + [(d, xm), (d, ym)]
    for peer in peers:
        pl.semaphore_signal(barrier, inc=1, device_id=peer, device_id_type=pl.DeviceIdType.MESH)
    pl.semaphore_wait(barrier, len(peers))

    def send(source, target, send_sem, recv_sem, device):
        return pltpu.make_async_remote_copy(
            src_ref=source, dst_ref=target, send_sem=send_sem, recv_sem=recv_sem,
            device_id=device, device_id_type=pl.DeviceIdType.MESH,
        )

    def rows(k):
        return pl.ds(k * block, block)

    def z_copy(k):
        target = flipped(d, k)
        return send(
            vis_ref.at[target], gathered.at[m, rows(k)], z_send.at[k], z_recv.at[k], (target, m)
        )

    def x_copy(k):
        mine = gathered.at[m, rows(k)]
        return send(mine, mine, x_send.at[k], x_recv.at[k], (d, xm))

    def y_copy(k):
        mine = gathered.at[m, rows(k)]
        return send(mine, mine, y_send.at[k], y_recv.at[k], (d, ym))

    def relays(k):
        half = features // 2
        both = k == n - 1
        copies = []
        if both or k % 2 == 0:
            part = gathered.at[xm, rows(k), pl.ds(0, half if both else features)]
            copies.append(send(part, part, d_send.at[k], d_recv.at[k], (d, ym)))
        if both or k % 2 == 1:
            start = half if both else 0
            part = gathered.at[ym, rows(k), pl.ds(start, features - start)]
            slot = n if both else k
            copies.append(send(part, part, d_send.at[slot], d_recv.at[slot], (d, xm)))
        return copies

    def spread(k):
        if k > 0:
            z_copy(k).wait_recv()
        x_copy(k).start()
        y_copy(k).start()

    def pass_on(k):
        if k % 2 == 0 or k == n - 1:
            x_copy(k).wait_recv()
        if k % 2 == 1 or k == n - 1:
            y_copy(k).wait_recv()
        for copy in relays(k):
            copy.start()

    def normalize(k):
        if k < n - 1:
            (y_copy if k % 2 == 0 else x_copy)(k).wait_recv()
        for copy in relays(k):
            copy.wait_recv()
        parts = gathered.shape[0]

        def piece(i, carry):
            here = pl.ds(pl.multiple_of(k * block + i * 16, 16), 16)
            total = jnp.zeros((16, 1), jnp.float32)
            for q in range(parts):
                total += jnp.sum(gathered[q, here].astype(jnp.float32), axis=-1, keepdims=True)
            average = total / (parts * features)
            spread_of = jnp.zeros((16, 1), jnp.float32)
            for q in range(parts):
                centred = gathered[q, here].astype(jnp.float32) - average
                spread_of += jnp.sum(centred * centred, axis=-1, keepdims=True)
            scale = lax.rsqrt(spread_of / (parts * features) + epsilon)
            for q in range(parts):
                span = slice(q * features, (q + 1) * features)
                centred = gathered[q, here].astype(jnp.float32) - average
                normed[here, span] = (centred * scale * vis_gain_ref[:, span]).astype(jnp.bfloat16)
            return carry

        lax.fori_loop(0, block // 16, piece, 0)

    gathered[m, rows(0)] = vis_ref[d]
    spread(0)
    for k in range(1, n):
        z_copy(k).start()

    tile = min(256, columns)
    tiles = columns // tile

    def tile_at(j):
        return pl.ds(pl.multiple_of(j * tile, tile), tile)

    def text_piece(i, carry):
        here = pl.ds(pl.multiple_of(i * 16, 16), 16)
        piece = text_ref[here].astype(jnp.float32)
        mean = jnp.mean(piece * piece, axis=-1, keepdims=True)
        text_norm[here] = (piece * lax.rsqrt(mean + epsilon) * text_gain_ref[...]).astype(
            jnp.bfloat16
        )
        return carry

    def query_tile(j, carry):
        queries[:, tile_at(j)] = jnp.dot(
            text_norm[...], wq[:, tile_at(j)], preferred_element_type=jnp.float32
        ).astype(jnp.bfloat16)
        return carry

    def kv_tiles(span):
        def one(j, carry):
            keys[span, tile_at(j)] = jnp.dot(
                normed[span], wk[:, tile_at(j)], preferred_element_type=jnp.float32
            ).astype(jnp.bfloat16)
            values[span, tile_at(j)] = jnp.dot(
                normed[span], wv[:, tile_at(j)], preferred_element_type=jnp.float32
            ).astype(jnp.bfloat16)
            return carry

        return one

    spread(1)
    loads[0].wait()
    lax.fori_loop(0, text_ref.shape[0] // 16, text_piece, 0)
    pass_on(0)
    for k in range(2, n):
        spread(k)
        pass_on(k - 1)
        if k == 2:
            loads[1].wait()
        lower, upper = (k - 2) * tiles // (n - 2), (k - 1) * tiles // (n - 2)
        if n == 2:
            lower, upper = 0, tiles
        if upper > lower:
            lax.fori_loop(lower, upper, query_tile, 0)
        if k >= n // 2 + 1:
            normalize(k - n // 2 - 1)
    if n == 2:
        loads[1].wait()
        lax.fori_loop(0, tiles, query_tile, 0)
    half = n // 2
    for k in range(half):
        if k < n // 2 + 1 and not (n > 2 and k <= n - 1 - n // 2 - 1):
            normalize(k)
    loads[2].wait()
    loads[3].wait()
    first, second = pl.ds(0, half * block), pl.ds(half * block, half * block)
    lax.fori_loop(0, tiles // 2, kv_tiles(first), 0)
    pass_on(n - 1)
    lax.fori_loop(tiles // 2, tiles, kv_tiles(first), 0)
    for k in range(half, n):
        normalize(k)
    lax.fori_loop(0, tiles, kv_tiles(second), 0)

    for h in range(columns // HEAD_DIM):
        span = slice(h * HEAD_DIM, (h + 1) * HEAD_DIM)
        scores = lax.dot_general(
            queries[:, span], keys[:, span], (((1,), (1,)), ((), ())),
            preferred_element_type=jnp.float32,
        ) * (HEAD_DIM ** -0.5)
        weights = jnp.exp(scores - jnp.max(scores, axis=-1, keepdims=True))
        total = jnp.sum(weights, axis=-1, keepdims=True)
        mixed = jnp.dot(
            weights.astype(jnp.bfloat16), values[:, span], preferred_element_type=jnp.float32
        )
        context[:, span] = (mixed / total).astype(jnp.bfloat16)

    loads[4].wait()

    def order(c):
        if c % 2 == 0:
            return x, y, (d, xm), (d, ym)
        return y, x, (d, ym), (d, xm)

    def first_copy(c):
        a, _, near, _ = order(c)
        return send(partial.at[c, 1 - a], first_in.at[c], s1_send.at[c], s1_recv.at[c], near)

    def second_copy(c):
        return send(second_out.at[c], second_in.at[c], s2_send.at[c], s2_recv.at[c], order(c)[3])

    def project(c):
        product = jnp.dot(
            context[...], wo[:, c * chunk : (c + 1) * chunk], preferred_element_type=jnp.float32
        ).astype(jnp.bfloat16)
        for r in range(4):
            a, b = (r % 2, r // 2) if c % 2 == 0 else (r // 2, r % 2)
            partial[c, a, b] = product[r * out_rows : (r + 1) * out_rows]
        first_copy(c).start()

    def turn(c):
        a, b, _, _ = order(c)
        first_copy(c).wait_recv()
        second_out[c] = (
            partial[c, a, 1 - b].astype(jnp.float32) + first_in[c, 1 - b].astype(jnp.float32)
        ).astype(jnp.bfloat16)
        second_copy(c).start()

    def finish(c):
        a, b, _, _ = order(c)
        second_copy(c).wait_recv()
        span = slice(c * chunk, (c + 1) * chunk)
        residual = text_ref[pl.ds(pl.multiple_of(m * out_rows, 16), out_rows), span]
        out_ref[:, span] = (
            residual.astype(jnp.float32)
            + partial[c, a, b].astype(jnp.float32)
            + first_in[c, b].astype(jnp.float32)
            + second_in[c].astype(jnp.float32)
        ).astype(jnp.bfloat16)

    for c in range(chunks):
        project(c)
        if c >= 3:
            turn(c - 3)
    for c in range(max(chunks - 3, 0), chunks):
        turn(c)
    for c in range(chunks):
        finish(c)

    for k in range(n):
        if k > 0:
            z_copy(k).wait_send()
        x_copy(k).wait_send()
        y_copy(k).wait_send()
        for copy in relays(k):
            copy.wait_send()
    for c in range(chunks):
        first_copy(c).wait_send()
        second_copy(c).wait_send()


def fused_body(n, visual, vis_gain, text, text_gain, query_weight, key_weight, value_weight, out_weight):
    block, _, features = visual.shape
    tokens, _, width = text.shape
    columns = key_weight.shape[1]
    vis_rows, vis_width = block * n, features * 4
    out_rows = tokens // 4
    chunks = 8
    chunk = width // chunks
    bf16 = jnp.bfloat16
    sems = [pltpu.SemaphoreType.DMA((5,))]
    sems += [pltpu.SemaphoreType.DMA((n,))] * 6 + [pltpu.SemaphoreType.DMA((n + 1,))] * 2
    sems += [pltpu.SemaphoreType.DMA((chunks,))] * 4
    vmem = pl.BlockSpec(memory_space=pltpu.VMEM)
    anywhere = pl.BlockSpec(memory_space=pl.ANY)
    result = pl.pallas_call(
        functools.partial(fused_kernel, n),
        out_shape=jax.ShapeDtypeStruct((out_rows, width), bf16),
        in_specs=[vmem] * 3 + [anywhere] * 5,
        out_specs=vmem,
        scratch_shapes=[
            pltpu.VMEM((4, vis_rows, features), bf16),
            pltpu.VMEM((vis_rows, vis_width), bf16),
            pltpu.VMEM((tokens, width), bf16),
            pltpu.VMEM((tokens, width), bf16),
            pltpu.VMEM(query_weight.shape, bf16),
            pltpu.VMEM(key_weight.shape, bf16),
            pltpu.VMEM(value_weight.shape, bf16),
            pltpu.VMEM(out_weight.shape, bf16),
            pltpu.VMEM((tokens, columns), bf16),
            pltpu.VMEM((vis_rows, columns), bf16),
            pltpu.VMEM((vis_rows, columns), bf16),
            pltpu.VMEM((tokens, columns), bf16),
            pltpu.VMEM((chunks, 2, 2, out_rows, chunk), bf16),
            pltpu.VMEM((chunks, 2, out_rows, chunk), bf16),
            pltpu.VMEM((chunks, out_rows, chunk), bf16),
            pltpu.VMEM((chunks, out_rows, chunk), bf16),
        ]
        + sems,
        compiler_params=pltpu.CompilerParams(
            collective_id=0, has_side_effects=True, vmem_limit_bytes=63 * 2**20
        ),
    )(
        jnp.transpose(visual, (1, 0, 2)),
        vis_gain.reshape(1, vis_width),
        text_gain.reshape(1, width),
        text.reshape(tokens, width),
        query_weight,
        key_weight,
        value_weight,
        out_weight,
    )
    return result.reshape(out_rows, 1, width)


def body(visual, *rest):
    n, groups = lax.axis_size("dp"), lax.axis_size("mp")
    text, columns = rest[1], rest[4].shape[1]
    block, images, features = visual.shape
    fits = (
        groups == 4
        and n >= 2
        and n & (n - 1) == 0
        and images == n
        and block % 16 == 0
        and features % 256 == 0
        and columns % HEAD_DIM == 0
        and (columns < 256 or columns % 256 == 0)
        and text.shape[0] % 64 == 0
        and text.shape[2] % 1024 == 0
    )
    if fits:
        return fused_body(n, visual, *rest)
    return plain_body(visual, *rest)


def solution(mesh):
    in_specs = (
        P("dp", None, "mp"),
        P(),
        P(None, "dp", None),
        P(),
        P(None, "mp"),
        P(None, "mp"),
        P(None, "mp"),
        P("mp", None),
    )
    out_specs = P("mp", "dp", None)
    return jax.shard_map(body, mesh=mesh, in_specs=in_specs, out_specs=out_specs, check_vma=False)
```
